512 devices in a mesh: ens: 8 (over z_lo, core), sp: 64 (over y, z_hi, x).
Axes of the slice: x: 4, y: 4, z: 16 (z_hi: 4, z_lo: 4; z = z_hi * 4 + z_lo), core: 2. Of those that a mesh axis runs over, the one named last changes fastest.
Arguments:
- tokens: bfloat16 [8, 128, 384, 768], P('ens', 'sp'), may hold values from -6 to 6
- cotangent: bfloat16 [8, 128, 384, 768], P('ens', 'sp'), may hold values from -6 to 6
- w_first: bfloat16 [768, 192], replicated, may hold values from -0.4375 to 0.4375
- b_first: bfloat16 [2, 768], replicated, may hold values from -3 to 3
- w_second: bfloat16 [768, 192], replicated, may hold values from -0.4375 to 0.4375
- b_second: bfloat16 [2, 768], replicated, may hold values from -3 to 3
Outputs:
- grad_tokens: bfloat16 [8, 128, 384, 768], P('ens', 'sp')
- grad_w_first: float32 [768, 192], P('sp')
- grad_b_first: float32 [2, 768], P(None, 'sp')
- grad_w_second: float32 [768, 192], P('sp')
- grad_b_second: float32 [2, 768], P(None, 'sp')
The draws below stay inside these ranges and needn't reach their ends.
All inputs are finite; a program needn't handle non-finite values.
Results may differ from the reference program's by a relative error of at most 0.022.
Values may be sent and summed in bfloat16 or wider, within the bound.
A program may use at most 64 MiB of HBM per device.

```python
import jax
import jax.numpy as jnp
from jax import lax

C = 768
NB = 8
BS = 96
W = 384
KW = 128
H = 128
E = 8
ROWS = 131072


def shard_levels(rng, dims, pieces, smallest, largest):
    factor_of, own = 1.0, jax.random.fold_in(rng, 6)
    for dim, parts in pieces:
        steps = jnp.exp(jax.random.uniform(jax.random.fold_in(own, dim), (parts,), jnp.float32, smallest / len(pieces), largest / len(pieces)))
        factor_of = factor_of * jnp.repeat(steps, dims[dim] // parts).reshape([-1 if axis == dim else 1 for axis in range(len(dims))])
    return factor_of


def normal_values(rng, shape, deviation, bound, pieces=(), kind=jnp.bfloat16):
    gain = shard_levels(rng, shape, pieces, -0.22, 0.18) if pieces else 1.0
    result = jax.random.normal(rng, shape, jnp.float32) * deviation * gain
    return jnp.minimum(jnp.maximum(result, -bound), bound).astype(kind)


def setup_inputs(seed: int = 0) -> dict:
    seeds = jax.random.split(jax.random.key(seed), 7)
    return {
        "tokens": normal_values(seeds[0], (E, H, W, C), 1.0, 6.0, ((0, 8), (1, 64))),
        "cotangent": normal_values(seeds[1], (E, H, W, C), 1.0, 6.0, ((0, 8), (1, 64))),
        "w_first": normal_values(seeds[2], (C, 2 * BS), (2 * BS) ** -0.5, 0.4375),
        "b_first": normal_values(seeds[3], (2, C), 0.5, 3.0),
        "w_second": normal_values(seeds[4], (C, 2 * BS), (2 * BS) ** -0.5, 0.4375),
        "b_second": normal_values(seeds[5], (2, C), 0.5, 3.0),
    }


shrink_level = 0.01
exact = lax.Precision.HIGHEST

def lon_tables(modes, points):
    wave = jnp.arange(modes, dtype=jnp.int32)[:, None]
    place = jnp.arange(points, dtype=jnp.int32)[None, :]
    angle = (wave * place % points).astype(jnp.float32) * (2.0 * jnp.pi / points)
    scale = 1.0 / jnp.sqrt(jnp.float32(points))
    paired = jnp.stack([jnp.cos(angle), -jnp.sin(angle)]) * scale
    doubled = jnp.where(wave == 0, 1.0, 2.0).astype(jnp.float32)
    return (paired, paired * doubled)

def lat_table(count):
    wave = jnp.arange(count, dtype=jnp.int32)[:, None]
    place = jnp.arange(count, dtype=jnp.int32)[None, :]
    angle = (wave * place % count).astype(jnp.float32) * (2.0 * jnp.pi / count)
    scale = 1.0 / jnp.sqrt(jnp.float32(count))
    cosine = jnp.cos(angle) * scale
    sine = jnp.sin(angle) * scale
    return jnp.stack([jnp.stack([cosine, sine], axis=1), jnp.stack([-sine, cosine], axis=1)])

def product(form, left, right):
    return jnp.einsum(form, left.astype(jnp.float32), right.astype(jnp.float32), precision=exact)

def complex_mix(left, weight):
    rows = left.shape[1]
    mixed = product('prnb,nbq->prnq', left.reshape(2, rows, NB, BS), weight.reshape(NB, BS, 2 * BS))
    real_part = mixed[0, :, :, :BS] - mixed[1, :, :, BS:]
    imag_part = mixed[0, :, :, BS:] + mixed[1, :, :, :BS]
    return jnp.stack([real_part, imag_part]).reshape(2, rows, C)

def pair_grads(grad):
    rows = grad.shape[1]
    split = grad.reshape(2, rows, NB, BS)
    return jnp.stack([jnp.concatenate([split[0], split[1]], axis=-1), jnp.concatenate([split[1], -split[0]], axis=-1)])

def back_mix(paired, weight):
    rows = paired.shape[1]
    return product('prnq,nbq->prnb', paired, weight.reshape(NB, BS, 2 * BS)).reshape(2, rows, C)

def weight_grad(left, paired):
    rows = left.shape[1]
    return product('prnb,prnq->nbq', left.reshape(2, rows, NB, BS), paired).reshape(C, 2 * BS)

def reference(tokens, cotangent, w_first, b_first, w_second, b_second):
    fwd_exact, inv_exact = lon_tables(KW, W)
    lat_exact = lat_table(H)
    lon_fwd = fwd_exact.astype(jnp.bfloat16)
    lon_inv = inv_exact.astype(jnp.bfloat16)
    lat_tab = lat_exact.astype(jnp.bfloat16)
    count = H * KW

    def member(carry, inputs):
        field, grad_out = inputs
        lon_spec = product('pkw,hwc->hpkc', fwd_exact, field)
        spectrum = product('pmqh,hqkc->pmkc', lat_exact, lon_spec).reshape(2, count, C)
        first_pre = complex_mix(spectrum, w_first) + b_first.astype(jnp.float32)[:, None, :]
        first_out = jnp.maximum(first_pre, 0.0)
        second_pre = complex_mix(first_out, w_second) + b_second.astype(jnp.float32)[:, None, :]
        cot_lon = product('pkw,hwc->hpkc', lon_inv, grad_out).astype(jnp.bfloat16)
        cot_spec = product('pmqh,hqkc->pmkc', lat_tab, cot_lon).reshape(2, count, C)
        grad_second = jnp.where(jnp.abs(second_pre) > shrink_level, cot_spec, 0.0).astype(jnp.bfloat16)
        paired_second = pair_grads(grad_second)
        grad_first = jnp.where(first_pre > 0.0, back_mix(paired_second, w_second), 0.0).astype(jnp.bfloat16)
        paired_first = pair_grads(grad_first)
        grad_spec = back_mix(paired_first, w_first).astype(jnp.bfloat16).reshape(2, H, KW, C)
        grad_lat = product('pmqh,pmkc->hqkc', lat_tab, grad_spec).astype(jnp.bfloat16)
        branch = product('pkw,hpkc->hwc', lon_fwd, grad_lat)
        grad_field = (grad_out.astype(jnp.float32) + branch).astype(jnp.bfloat16)
        terms = (weight_grad(spectrum, paired_first), lax.optimization_barrier(jnp.sum(grad_first.astype(jnp.float32), axis=1)), weight_grad(first_out, paired_second), lax.optimization_barrier(jnp.sum(grad_second.astype(jnp.float32), axis=1)))
        return (tuple((held + term for held, term in zip(carry, terms))), grad_field)
    start = (jnp.zeros((C, 2 * BS), jnp.float32), jnp.zeros((2, C), jnp.float32), jnp.zeros((C, 2 * BS), jnp.float32), jnp.zeros((2, C), jnp.float32))
    totals, grad_tokens = lax.scan(member, start, (tokens, cotangent))
    factor = float(ROWS) ** (-0.5)
    return (grad_tokens, totals[0] * factor, totals[1] * factor, totals[2] * factor, totals[3] * factor)
```

```python
import functools

import jax
import jax.numpy as jnp
import ml_dtypes
import numpy as np
from jax import lax
from jax.experimental import pallas as pl
from jax.experimental.pallas import tpu as pltpu
from jax.sharding import PartitionSpec as P

MESH = pl.DeviceIdType.MESH
BF = jnp.bfloat16
F32 = jnp.float32
LEVEL = 0.01
CODE_SPAN = 249.0
CODE_BASE = 124.0
FACTOR = float(131072) ** (-0.5)


def constants():
    k = np.arange(128)[:, None]
    w = np.arange(384)[None, :]
    a = 2.0 * np.pi * ((k * w) % 384) / 384.0
    lon = (np.stack([np.cos(a), -np.sin(a)]) / np.sqrt(384.0)).astype(np.float32)
    lon = lon.reshape(2, 32, 4, 384).transpose(1, 0, 2, 3).reshape(256, 384)
    m = np.arange(128)[:, None]
    h = np.arange(128)[None, :]
    b = 2.0 * np.pi * ((m * h) % 128) / 128.0
    c, s = np.cos(b) / np.sqrt(128.0), np.sin(b) / np.sqrt(128.0)
    lat = np.stack([np.stack([c, s], 2), np.stack([-s, c], 2)])
    lat = lat.astype(np.float32).reshape(256, 256)

    def split(t):
        hi = t.astype(ml_dtypes.bfloat16)
        return hi, (t - hi.astype(np.float32)).astype(ml_dtypes.bfloat16)

    lon_hi, lon_lo = split(lon)
    lat_hi, lat_lo = split(lat)
    place = np.zeros((2, 2, 4, 2, 16, 384), np.float32)
    for yy in range(2):
        for z in range(4):
            for x in range(4):
                for r in range(12):
                    place[yy, z // 2, x, z % 2, r, yy * 192 + z * 48 + x * 12 + r] = 1.0
    place = place.reshape(512, 384).astype(ml_dtypes.bfloat16)
    return [lon_hi, lon_lo, np.ascontiguousarray(lon_hi.T), lat_hi, lat_lo, np.ascontiguousarray(lat_hi.T), place]


def dot(a, b):
    return lax.dot_general(a, b, (((1,), (0,)), ((), ())), preferred_element_type=F32)


def dot_t(a, b):
    return lax.dot_general(a, b, (((1,), (1,)), ((), ())), preferred_element_type=F32)


def halves(x):
    hi = x.astype(BF)
    return hi, (x - hi.astype(F32)).astype(BF)


def iota(shape, dim):
    return lax.broadcasted_iota(jnp.int32, shape, dim)


def block_of(i):
    return (i >= 96).astype(jnp.int32) + (i >= 192).astype(jnp.int32) + (i >= 288).astype(jnp.int32)


def wide(s):
    return jnp.concatenate([s, s, s], axis=1)


def kernel(
    tok, cot, w1, b1, w2, b2, lon_hi, lon_lo, lon_t, lat_hi, lat_lo, lat_t, place,
    out, out_w,
    lonbuf, send_t, send_s, recv_t, recv_s, send_c, recv_c, send_g, recv_g,
    rows, xh, xl, spec_b, first_b, mask_b, g1_b, g2_b, v1, v2, r1, r2,
    send_a, recv_a, send_b, recv_b, send_e, recv_e, ss, rs,
):
    e = lax.axis_index("ens")
    me = lax.axis_index("sp")
    half = lax.div(me, 32)
    barrier = pltpu.get_barrier_semaphore()

    def greet(i, carry):
        pl.semaphore_signal(barrier, inc=1, device_id=(e, lax.rem(me + i, 64)), device_id_type=MESH)
        return carry

    def greet_ens(i, carry):
        pl.semaphore_signal(barrier, inc=1, device_id=(lax.rem(e + i, 8), me), device_id_type=MESH)
        return carry

    lax.fori_loop(1, 64, greet, 0)
    lax.fori_loop(1, 8, greet_ens, 0)

    def remote(src, dst, j, dev):
        return pltpu.make_async_remote_copy(
            src, dst, ss.at[j], rs.at[j], device_id=dev, device_id_type=MESH
        )

    def all_of(src, dst, j, n):
        return remote(src.at[pl.ds(0, n)], dst.at[pl.ds(0, n)], j, (e, lax.rem(me + 1, 64)))

    for h in range(2):
        for f in range(2):
            t = tok[h, :, f * 384 : (f + 1) * 384]
            lonbuf[f, h] = dot(lon_hi[...], t) + dot(lon_lo[...], t)
    pl.semaphore_wait(barrier, 70)

    def pair(d):
        f, g = lax.div(d, 32), pl.multiple_of(lax.rem(d, 32) * 8, 8)
        return jnp.concatenate([lonbuf[f, 0, pl.ds(g, 8), :], lonbuf[f, 1, pl.ds(g, 8), :]], axis=0)

    def code(d):
        z = pair(d)
        az = jnp.abs(z)
        top = jnp.max(az, axis=0, keepdims=True)
        top = jnp.maximum(jnp.maximum(top[:, :128], top[:, 128:256]), top[:, 256:])
        top = jnp.maximum(top, 1e-30)
        y = jnp.exp2(az * wide(CODE_SPAN / top) - CODE_BASE)
        return jnp.where(z < 0.0, -y, y).astype(BF), top

    def send_tok(i, carry):
        d = lax.rem(me + i, 64)
        y, top = code(d)
        send_t[d] = y
        send_s[d] = top
        remote(send_t.at[d], recv_t.at[me], 0, (e, d)).start()
        remote(send_s.at[d], recv_s.at[me], 1, (e, d)).start()
        return carry

    lax.fori_loop(1, 64, send_tok, 0)
    y, top = code(me)
    recv_t[me] = y
    recv_s[me] = top

    row = iota((256, 384), 0)
    scale = jnp.where((row == 0) | (row == 4), 1.0, 2.0)
    for h in range(2):
        for f in range(2):
            lonbuf[f, h] = dot(lon_hi[...], cot[h, :, f * 384 : (f + 1) * 384]) * scale

    def send_cot(i, carry):
        d = lax.rem(me + i, 64)
        send_c[d] = pair(d).astype(BF)
        remote(send_c.at[d], recv_c.at[me], 2, (e, d)).start()
        return carry

    lax.fori_loop(1, 64, send_cot, 0)
    recv_c[me] = pair(me).astype(BF)

    q, j = iota((192, 768), 0), iota((192, 768), 1)
    jm = jnp.where(j >= 384, j - 384, j)
    inner = jm - 96 * block_of(jm) + jnp.where(j >= 384, 96, 0)
    spread = jnp.where(q == inner, 1.0, 0.0).astype(BF)
    r, j = iota((384, 768), 0), iota((384, 768), 1)
    own = block_of(r) == block_of(jnp.where(j >= 384, j - 384, j))
    here = pl.ds(pl.multiple_of(half * 384, 384), 384)
    v1[...] = jnp.where(own, dot(w1[here, :], spread), 0.0).astype(BF)
    v2[...] = jnp.where(own, dot(w2[here, :], spread), 0.0).astype(BF)

    def bias(ref):
        t = ref[...].astype(F32)
        t = jnp.where(half == 0, t[:, :384], t[:, 384:])
        return t[0:1], t[1:2]

    b1r, b1i = bias(b1)
    b2r, b2i = bias(b2)

    all_of(send_t, recv_t, 0, 63).wait_recv()
    all_of(send_s, recv_s, 1, 63).wait_recv()

    def put_rows(i, x):
        for t in range(3):
            rows[t, pl.ds(pl.multiple_of(i * 16, 16), 16), :] = x[:, 128 * t : 128 * (t + 1)]

    def mode_rows(k):
        return jnp.concatenate([rows[t, pl.ds(k, 256, stride=4), :] for t in range(3)], axis=1)

    def decode(i, carry):
        y = recv_t[i].astype(F32)
        u = (jnp.log2(jnp.abs(y)) + CODE_BASE) * wide(recv_s[i] * (1.0 / CODE_SPAN))
        put_rows(i, jnp.where(y < 0.0, -u, u))
        return carry

    lax.fori_loop(0, 64, decode, 0)
    for k in range(4):
        hi, lo = halves(mode_rows(k))
        xh[k] = hi
        xl[k] = lo

    def mix(x, v, br, bi):
        hi, lo = halves(x)
        t = dot(hi, v[...]) + dot(lo, v[...])
        real = t[:128, :384] - t[128:, 384:] + br
        imag = t[:128, 384:] + t[128:, :384] + bi
        return hi, jnp.concatenate([real, imag], axis=0)

    def forward(k, carry):
        s = dot(lat_hi[...], xh[k]) + dot(lat_hi[...], xl[k]) + dot(lat_lo[...], xh[k])
        hi, pre = mix(s, v1, b1r, b1i)
        spec_b[k] = hi
        hi, pre = mix(jnp.maximum(pre, 0.0), v2, b2r, b2i)
        first_b[k] = hi
        mask_b[k] = jnp.where(jnp.abs(pre) > LEVEL, 1.0, 0.0).astype(BF)
        return carry

    lax.fori_loop(0, 4, forward, 0)

    all_of(send_c, recv_c, 2, 63).wait_recv()

    def unpack(i, carry):
        put_rows(i, recv_c[i].astype(F32))
        return carry

    lax.fori_loop(0, 64, unpack, 0)
    for k in range(4):
        xh[k] = mode_rows(k).astype(BF)

    def back(g, v):
        br, bi = dot_t(g, v[:, :384]), dot_t(g, v[:, 384:])
        return jnp.concatenate([br[:128] + bi[128:], br[128:] - bi[:128]], axis=0)

    def backward(k, carry):
        g2 = jnp.where(mask_b[k].astype(F32) > 0.0, dot(lat_hi[...], xh[k]), 0.0).astype(BF)
        g2_b[k] = g2
        g1 = jnp.where(first_b[k].astype(F32) > 0.0, back(g2, v2), 0.0).astype(BF)
        g1_b[k] = g1
        lonbuf[lax.div(k, 2), lax.rem(k, 2)] = dot(lat_t[...], back(g1, v1).astype(BF))
        return carry

    lax.fori_loop(0, 4, backward, 0)
    for k in range(4):
        for t in range(3):
            rows[t, pl.ds(k, 256, stride=4), :] = lonbuf[k // 2, k % 2, :, 128 * t : 128 * (t + 1)]

    def grad_block(d):
        at = pl.ds(pl.multiple_of(d * 16, 16), 16)
        return jnp.concatenate([rows[t, at, :] for t in range(3)], axis=1).astype(BF)

    def send_grad(i, carry):
        d = lax.rem(me + i, 64)
        send_g[d] = grad_block(d)
        remote(send_g.at[d], recv_g.at[me], 3, (e, d)).start()
        return carry

    lax.fori_loop(1, 64, send_grad, 0)
    recv_g[me] = grad_block(me)

    r1[...] = jnp.zeros_like(r1)
    r2[...] = jnp.zeros_like(r2)
    slot, col = iota((512, 256), 0), iota((512, 256), 1)
    ones = jnp.where((jnp.bitwise_and(slot, 15) == 12) & (col < 128), 1.0, 0.0)

    def outer(left, g):
        lt = (dot_t(place[...], left) + ones).astype(BF)
        swapped = jnp.concatenate([g[128:], -g[:128]], axis=0)
        return dot(lt, g), dot(lt, swapped)

    def weights(k, carry):
        a, b = outer(spec_b[k], g1_b[k])
        r1[:, :384] += a
        r1[:, 384:] += b
        a, b = outer(first_b[k], g2_b[k])
        r2[:, :384] += a
        r2[:, 384:] += b
        return carry

    lax.fori_loop(0, 4, weights, 0)

    def fold(n, part, ref):
        lane, to = iota((384, 384), 0), iota((384, 384), 1)
        total = 0.0
        for p in range(2):
            pick = jnp.where((lane - 96 * n == to - 192 * part - 96 * p) & (block_of(lane) == n), 1.0, 0.0).astype(BF)
            hi, lo = halves(ref[128 * n : 128 * (n + 1), 384 * p : 384 * (p + 1)])
            total = total + dot(hi, pick) + dot(lo, pick)
        return total

    for n in range(4):
        t = (fold(n, 0, r1) + fold(n, 1, r2)) * FACTOR
        send_a[4 * (n // 2) : 4 * (n // 2) + 4, n % 2] = t.reshape(4, 32, 384)

    x = lax.rem(me, 4)
    z = lax.rem(lax.div(me, 4), 4)
    mine = lax.rem(lax.div(me, 16), 2) * 4 + x

    def send_plane(i, carry):
        o = lax.rem(mine + i, 8)
        d = half * 32 + lax.div(o, 4) * 16 + z * 4 + lax.rem(o, 4)
        remote(send_a.at[o], recv_a.at[mine], 4, (e, d)).start()
        return carry

    lax.fori_loop(1, 8, send_plane, 0)
    recv_a[mine] = send_a[mine]
    all_of(send_a, recv_a, 4, 7).wait_recv()
    total = recv_a[0]
    for o in range(1, 8):
        total = total + recv_a[o]
    send_b[...] = total.reshape(4, 16, 384)

    def send_z(i, carry):
        o = lax.rem(z + i, 4)
        remote(send_b.at[o], recv_b.at[z], 5, (e, me + (o - z) * 4)).start()
        return carry

    lax.fori_loop(1, 4, send_z, 0)
    recv_b[z] = send_b[z]
    all_of(send_b, recv_b, 5, 3).wait_recv()
    total = recv_b[0] + recv_b[1] + recv_b[2] + recv_b[3]
    send_e[0] = total

    def send_ens(i, carry):
        remote(send_e.at[0], recv_e.at[e], 6, (lax.rem(e + i, 8), me)).start()
        return carry

    lax.fori_loop(1, 8, send_ens, 0)
    recv_e[e] = total
    all_of(recv_e, recv_e, 6, 7).wait_recv()
    total = recv_e[0]
    for o in range(1, 8):
        total = total + recv_e[o]
    out_w[...] = total

    all_of(send_g, recv_g, 3, 63).wait_recv()
    for f in range(2):
        t = recv_g[32 * f : 32 * (f + 1)].astype(F32)
        for h in range(2):
            g = t[:, 8 * h : 8 * (h + 1), :].reshape(256, 384).astype(BF)
            branch = dot(lon_t[...], g)
            lanes = slice(384 * f, 384 * (f + 1))
            out[h, :, lanes] = (cot[h, :, lanes].astype(F32) + branch).astype(BF)

    all_of(send_t, recv_t, 0, 63).wait_send()
    all_of(send_s, recv_s, 1, 63).wait_send()
    all_of(send_c, recv_c, 2, 63).wait_send()
    all_of(send_g, recv_g, 3, 63).wait_send()
    all_of(send_a, recv_a, 4, 7).wait_send()
    all_of(send_b, recv_b, 5, 3).wait_send()
    all_of(recv_e, recv_e, 6, 7).wait_send()


def shards(tables, tokens, cotangent, w_first, b_first, w_second, b_second):
    blocks = lambda n, kind: pltpu.VMEM((n, 16, 384), kind)
    parts = lambda kind: pltpu.VMEM((4, 256, 384), kind)
    scratch = [
        pltpu.VMEM((2, 2, 256, 384), F32),
        blocks(64, BF), pltpu.VMEM((64, 1, 128), F32), blocks(64, BF), pltpu.VMEM((64, 1, 128), F32),
        blocks(64, BF), blocks(64, BF), blocks(64, BF), blocks(64, BF),
        pltpu.VMEM((3, 1024, 128), F32),
        parts(BF), parts(BF), parts(BF), parts(BF), parts(BF), parts(BF), parts(BF),
        pltpu.VMEM((384, 768), BF), pltpu.VMEM((384, 768), BF),
        pltpu.VMEM((512, 768), F32), pltpu.VMEM((512, 768), F32),
        pltpu.VMEM((8, 2, 32, 384), F32), pltpu.VMEM((8, 2, 32, 384), F32),
        blocks(4, F32), blocks(4, F32), blocks(1, F32), blocks(8, F32),
        pltpu.SemaphoreType.DMA((7,)), pltpu.SemaphoreType.DMA((7,)),
    ]
    spec = pl.BlockSpec(memory_space=pltpu.VMEM)
    field, grads = pl.pallas_call(
        kernel,
        out_shape=(jax.ShapeDtypeStruct((2, 384, 768), BF), jax.ShapeDtypeStruct((16, 384), F32)),
        in_specs=[spec] * 13,
        out_specs=(spec, spec),
        scratch_shapes=scratch,
        name="afno_backward",
        compiler_params=pltpu.CompilerParams(
            collective_id=0, has_side_effects=True, vmem_limit_bytes=48 << 20
        ),
    )(tokens[0], cotangent[0], w_first, b_first, w_second, b_second, *[jnp.asarray(t) for t in tables])
    at = lax.rem(lax.axis_index("sp"), 8) * 12
    sums = grads[12].reshape(2, 2, 96)
    sums = lax.dynamic_slice_in_dim(sums, at, 12, 2)
    return field[None], grads[:12, :192], sums[0], grads[:12, 192:], sums[1]


def solution(mesh):
    return jax.shard_map(
        functools.partial(shards, constants()),
        mesh=mesh,
        in_specs=(P("ens", "sp", None, None), P("ens", "sp", None, None), P(), P(), P(), P()),
        out_specs=(
            P("ens", "sp", None, None),
            P("sp", None),
            P(None, "sp"),
            P("sp", None),
            P(None, "sp"),
        ),
        check_vma=False,
    )
```

```python
import functools

import jax
import jax.numpy as jnp
import ml_dtypes
import numpy as np
from jax import lax
from jax.experimental import pallas as pl
from jax.experimental.pallas import tpu as pltpu
from jax.sharding import PartitionSpec as P

MESH = pl.DeviceIdType.MESH
BF = jnp.bfloat16
F32 = jnp.float32
LEVEL = 0.01
CODE_SPAN = 249.0
CODE_BASE = 124.0
FACTOR = float(131072) ** (-0.5)
WINDOWS = (0, 0, 128, 128)


def constants():
    k = np.arange(128)[:, None]
    w = np.arange(384)[None, :]
    a = 2.0 * np.pi * ((k * w) % 384) / 384.0
    lon = (np.stack([np.cos(a), -np.sin(a)]) / np.sqrt(384.0)).astype(np.float32)
    lon = lon.reshape(2, 32, 4, 384).transpose(1, 0, 2, 3).reshape(256, 384)
    m = np.arange(128)[:, None]
    h = np.arange(128)[None, :]
    b = 2.0 * np.pi * ((m * h) % 128) / 128.0
    c, s = np.cos(b) / np.sqrt(128.0), np.sin(b) / np.sqrt(128.0)
    lat = np.stack([np.stack([c, s], 2), np.stack([-s, c], 2)])
    lat = lat.astype(np.float32).reshape(256, 256)

    def split(t):
        hi = t.astype(ml_dtypes.bfloat16)
        return hi, (t - hi.astype(np.float32)).astype(ml_dtypes.bfloat16)

    lon_hi, lon_lo = split(lon)
    lat_hi, lat_lo = split(lat)
    place = np.zeros((2, 2, 4, 2, 16, 384), np.float32)
    for yy in range(2):
        for z in range(4):
            for x in range(4):
                for r in range(12):
                    place[yy, z // 2, x, z % 2, r, yy * 192 + z * 48 + x * 12 + r] = 1.0
    place = place.reshape(512, 384).astype(ml_dtypes.bfloat16)
    return [lon_hi, lon_lo, np.ascontiguousarray(lon_hi.T), lat_hi, lat_lo, np.ascontiguousarray(lat_hi.T), place]


def dot(a, b):
    return lax.dot_general(a, b, (((1,), (0,)), ((), ())), preferred_element_type=F32)


def dot_t(a, b):
    return lax.dot_general(a, b, (((1,), (1,)), ((), ())), preferred_element_type=F32)


def halves(x):
    hi = x.astype(BF)
    return hi, (x - hi.astype(F32)).astype(BF)


def iota(shape, dim):
    return lax.broadcasted_iota(jnp.int32, shape, dim)


def block_of(i):
    return (i >= 96).astype(jnp.int32) + (i >= 192).astype(jnp.int32) + (i >= 288).astype(jnp.int32)


def wide(s):
    return jnp.concatenate([s, s, s], axis=1)


def kernel(
    tok_a, cot_a, w1_a, b1_a, w2_a, b2_a, lon_hi_a, lon_lo_a, lon_t_a, lat_hi_a, lat_lo_a, lat_t_a, place_a,
    out, out_w,
    tok, cot, w1, b1, w2, b2, lon_hi, lon_lo, lon_t, lat_hi, lat_lo, lat_t, place, load,
    lonbuf, send_t, send_s, recv_t, recv_s, send_cx, recv_cx, send_cy, recv_cy, send_g0, recv_g0, send_g1, recv_g1, middle,
    rows, xh, xl, first_b, mask_b, g1_b, g2_b, v1, v2, left1, left2, pick,
    send_a, recv_a, send_b, recv_b, send_e, recv_e, ss, rs,
):
    pairs = [
        (lon_hi_a, lon_hi), (lon_lo_a, lon_lo), (tok_a, tok), (cot_a, cot), (w1_a, w1), (b1_a, b1), (w2_a, w2),
        (b2_a, b2), (lat_hi_a, lat_hi), (lat_lo_a, lat_lo), (lat_t_a, lat_t), (place_a, place), (lon_t_a, lon_t),
    ]
    loads = [pltpu.make_async_copy(a, b, load.at[n]) for n, (a, b) in enumerate(pairs)]
    for copy in loads:
        copy.start()
    e = lax.axis_index("ens")
    me = lax.axis_index("sp")
    half = lax.div(me, 32)
    barrier = pltpu.get_barrier_semaphore()

    def greet(i, carry):
        pl.semaphore_signal(barrier, inc=1, device_id=(e, lax.rem(me + i, 64)), device_id_type=MESH)
        return carry

    def greet_ens(i, carry):
        pl.semaphore_signal(barrier, inc=1, device_id=(lax.rem(e + i, 8), me), device_id_type=MESH)
        return carry

    lax.fori_loop(1, 64, greet, 0)
    lax.fori_loop(1, 8, greet_ens, 0)
    x = lax.rem(me, 4)
    y = lax.div(me, 16)
    z = lax.rem(lax.div(me, 4), 4)
    core = lax.rem(e, 2)
    mine = core * 8 + lax.rem(y, 2) * 4 + x

    def peer(o):
        j = lax.rem(o, 8)
        return (e - core + lax.div(o, 8), half * 32 + lax.div(j, 4) * 16 + z * 4 + lax.rem(j, 4))

    def greet_core(i, carry):
        o = (1 - core) * 8 + lax.rem(mine + i, 8)
        pl.semaphore_signal(barrier, inc=1, device_id=peer(o), device_id_type=MESH)
        return carry

    lax.fori_loop(1, 8, greet_core, 0)

    def remote(src, dst, j, dev):
        return pltpu.make_async_remote_copy(
            src, dst, ss.at[j], rs.at[j], device_id=dev, device_id_type=MESH
        )

    def all_of(src, dst, j, n):
        return remote(src.at[pl.ds(0, n)], dst.at[pl.ds(0, n)], j, (e, lax.rem(me + 1, 64)))

    for copy in loads[:3]:
        copy.wait()
    for h in range(2):
        for f in range(2):
            t = tok[h, :, f * 384 : (f + 1) * 384]
            lonbuf[f, h] = dot(lon_hi[...], t) + dot(lon_lo[...], t)
    pl.semaphore_wait(barrier, 77)

    def dest(i):
        return lax.rem(me + i, 64)

    def pair(buf, d):
        f, g = lax.div(d, 32), pl.multiple_of(lax.rem(d, 32) * 8, 8)
        return jnp.concatenate([buf[f, 0, pl.ds(g, 8), :], buf[f, 1, pl.ds(g, 8), :]], axis=0)

    def send_tok(i, carry):
        d = dest(i)
        v = pair(lonbuf, d)
        av = jnp.abs(v)
        top = jnp.max(av, axis=0, keepdims=True)
        top = jnp.maximum(jnp.maximum(top[:, :128], top[:, 128:256]), top[:, 256:])
        top = jnp.maximum(top, 1e-30)
        coded = jnp.exp2(av * wide(CODE_SPAN / top) - CODE_BASE)
        send_t[d] = jnp.where(v < 0.0, -coded, coded).astype(BF)
        send_s[d] = top

        @pl.when(d != me)
        def _():
            remote(send_t.at[d], recv_t.at[me], 0, (e, d)).start()
            remote(send_s.at[d], recv_s.at[me], 1, (e, d)).start()

        return carry

    def send_cot(part, i, carry):
        d = dest(i)
        src, dst = (send_cx, recv_cx) if part == 0 else (send_cy, recv_cy)
        v = pair(lonbuf, d)
        src[d] = (v[:, :256] if part == 0 else v[:, 256:]).astype(BF)

        @pl.when(d != me)
        def _():
            remote(src.at[d], dst.at[me], 2 + part, (e, d)).start()

        return carry

    lax.fori_loop(0, 64, send_tok, 0)
    recv_t[me] = send_t[me]
    recv_s[me] = send_s[me]
    loads[3].wait()
    row = iota((256, 384), 0)
    scale = jnp.where((row == 0) | (row == 4), 1.0, 2.0)
    for h in range(2):
        for g in range(2):
            lonbuf[g, h] = dot(lon_hi[...], cot[h, :, g * 384 : (g + 1) * 384]) * scale
    lax.fori_loop(0, 64, functools.partial(send_cot, 0), 0)
    lax.fori_loop(0, 64, functools.partial(send_cot, 1), 0)
    recv_cx[me] = send_cx[me]
    recv_cy[me] = send_cy[me]

    for copy in loads[4:]:
        copy.wait()
    q, j = iota((192, 768), 0), iota((192, 768), 1)
    jm = jnp.where(j >= 384, j - 384, j)
    inner = jm - 96 * block_of(jm) + jnp.where(j >= 384, 96, 0)
    spread = jnp.where(q == inner, 1.0, 0.0).astype(BF)
    r, j = iota((384, 768), 0), iota((384, 768), 1)
    own = block_of(r) == block_of(jnp.where(j >= 384, j - 384, j))

    def diagonal(w):
        t = jnp.where(half == 0, w[:, :384].astype(F32), w[:, 384:].astype(F32)).astype(BF)
        t = lax.dot_general(t, spread, (((0,), (0,)), ((), ())), preferred_element_type=F32)
        return jnp.where(own, t, 0.0).astype(BF)

    v1[...] = diagonal(w1)
    v2[...] = diagonal(w2)

    def bias(ref):
        t = ref[...].astype(F32)
        t = jnp.where(half == 0, t[:, :384], t[:, 384:])
        return t[0:1], t[1:2]

    lane, to = iota((256, 384), 0), iota((256, 384), 1)
    for n in range(4):
        for part in range(4):
            at = 96 * n - WINDOWS[n]
            inside = (lane >= at) & (lane < at + 96)
            pick[n, part] = jnp.where((lane - at == to - 96 * part) & inside, 1.0, 0.0).astype(BF)
    slot, col = iota((512, 256), 0), iota((512, 256), 1)
    ones = jnp.where((jnp.bitwise_and(slot, 15) == 12) & (col < 128), 1.0, 0.0)

    b1r, b1i = bias(b1)
    b2r, b2i = bias(b2)

    all_of(send_t, recv_t, 0, 63).wait_recv()
    all_of(send_s, recv_s, 1, 63).wait_recv()

    def put_rows(i, x):
        for t in range(3):
            rows[t, pl.ds(pl.multiple_of(i * 16, 16), 16), :] = x[:, 128 * t : 128 * (t + 1)]

    def mode_rows(k):
        return jnp.concatenate([rows[t, pl.ds(k, 256, stride=4), :] for t in range(3)], axis=1)

    def decode(i, carry):
        y = recv_t[i].astype(F32)
        u = (jnp.log2(jnp.abs(y)) + CODE_BASE) * wide(recv_s[i] * (1.0 / CODE_SPAN))
        put_rows(i, jnp.where(y < 0.0, -u, u))
        return carry

    lax.fori_loop(0, 64, decode, 0, unroll=4)
    for k in range(4):
        hi, lo = halves(mode_rows(k))
        xh[k] = hi
        xl[k] = lo

    low = iota((256, 128), 1) < 64

    def join(a, b):
        return jnp.concatenate([a[:, :128], jnp.where(low, a[:, 128:], b[:, :128]), b[:, 128:]], axis=1)

    def mix(x, v, br, bi):
        hi, lo = halves(x)

        def window(w, col):
            here = slice(128 * w, 128 * w + 256)
            vw = v[here, 384 * col + 128 * w : 384 * col + 128 * w + 256]
            return dot(hi[:, here], vw) + dot(lo[:, here], vw)

        tr = join(window(0, 0), window(1, 0))
        ti = join(window(0, 1), window(1, 1))
        real = tr[:128] - ti[128:] + br
        imag = ti[:128] + tr[128:] + bi
        return hi, jnp.concatenate([real, imag], axis=0)

    def forward(k, carry):
        s = dot(lat_hi[...], xh[k]) + dot(lat_hi[...], xl[k]) + dot(lat_lo[...], xh[k])
        hi, pre = mix(s, v1, b1r, b1i)
        left1[k] = (dot_t(place[...], hi) + ones).astype(BF)
        hi, pre = mix(jnp.maximum(pre, 0.0), v2, b2r, b2i)
        first_b[k] = hi
        left2[k] = (dot_t(place[...], hi) + ones).astype(BF)
        mask_b[k] = jnp.where(jnp.abs(pre) > LEVEL, 1.0, 0.0).astype(BF)
        return carry

    lax.fori_loop(0, 4, forward, 0)

    def unpack(part, i, carry):
        at = pl.ds(pl.multiple_of(i * 16, 16), 16)
        if part == 0:
            t = recv_cx[i].astype(F32)
            rows[0, at, :] = t[:, :128]
            rows[1, at, :] = t[:, 128:]
        else:
            rows[2, at, :] = recv_cy[i].astype(F32)
        return carry

    def back(g, v, w):
        here = slice(128 * w, 128 * w + 256)
        br = dot_t(g, v[here, here])
        bi = dot_t(g, v[here, 384 + 128 * w : 640 + 128 * w])
        return jnp.concatenate([br[:128] + bi[128:], br[128:] - bi[:128]], axis=0)

    def backward(k, w):
        here = slice(128 * w, 128 * w + 256)
        mine = slice(256 * k, 256 * (k + 1))
        g2 = jnp.where(mask_b[k, :, here].astype(F32) > 0.0, dot(lat_hi[...], xh[k, :, here]), 0.0).astype(BF)
        g2_b[mine, here] = g2
        g1 = jnp.where(first_b[k, :, here].astype(F32) > 0.0, back(g2, v2, w), 0.0).astype(BF)
        if w == 0:
            g1_b[mine, here] = g1
        else:
            g1_b[mine, 128:256] = jnp.where(low, g1_b[mine, 128:256].astype(F32), g1[:, :128].astype(F32)).astype(BF)
            g1_b[mine, 256:] = g1[:, 128:]
        return dot(lat_t[...], back(g1, v1, w).astype(BF))

    def send_grad(part, i, carry):
        d = dest(i)
        at = pl.ds(pl.multiple_of(d * 16, 16), 16)
        src, dst = (send_g0, recv_g0) if part == 0 else (send_g1, recv_g1)
        if part == 0:
            src[d] = rows[0, at, :].astype(BF)
        else:
            src[d] = jnp.concatenate([rows[1, at, :], rows[2, at, :]], axis=1).astype(BF)

        @pl.when(d != me)
        def _():
            remote(src.at[d], dst.at[me], 7 + part, (e, d)).start()

        return carry

    all_of(send_cx, recv_cx, 2, 63).wait_recv()
    lax.fori_loop(0, 64, functools.partial(unpack, 0), 0, unroll=4)
    for k in range(4):
        for t in range(2):
            xh[k, :, 128 * t : 128 * (t + 1)] = rows[t, pl.ds(k, 256, stride=4), :].astype(BF)
    for k in range(4):
        g = backward(k, 0)
        rows[0, pl.ds(k, 256, stride=4), :] = g[:, :128]
        middle[k] = g[:, 128:]
    lax.fori_loop(0, 64, functools.partial(send_grad, 0), 0)
    recv_g0[me] = send_g0[me]

    all_of(send_cy, recv_cy, 3, 63).wait_recv()
    lax.fori_loop(0, 64, functools.partial(unpack, 1), 0, unroll=4)
    for k in range(4):
        xh[k, :, 256:] = rows[2, pl.ds(k, 256, stride=4), :].astype(BF)
    for k in range(4):
        g = backward(k, 1)
        rows[1, pl.ds(k, 256, stride=4), :] = jnp.where(low, middle[k], g[:, :128])
        rows[2, pl.ds(k, 256, stride=4), :] = g[:, 128:]

    def outer(n, left, g):
        lanes = slice(WINDOWS[n], WINDOWS[n] + 256)
        real, imag = 0.0, 0.0
        for k in range(4):
            lt = left[k, 128 * n : 128 * (n + 1), :]
            gr, gi = g[256 * k : 256 * k + 128, lanes], g[256 * k + 128 : 256 * (k + 1), lanes]
            real = real + dot(lt, jnp.concatenate([gr, gi], axis=0))
            imag = imag + dot(lt, jnp.concatenate([gi, -gr], axis=0))
        return real, imag

    for n in range(4):
        total = 0.0
        for part, t in enumerate(outer(n, left1, g1_b) + outer(n, left2, g2_b)):
            hi, lo = halves(t)
            total = total + dot(hi, pick[n, part]) + dot(lo, pick[n, part])
        total = (total * FACTOR).reshape(4, 2, 2, 8, 384)
        for zl in range(2):
            for c in range(2):
                at = c * 8 + 4 * (n // 2)
                send_a[at : at + 4, 2 * (n % 2) + zl] = total[:, zl, c]

    def send_plane(i, carry):
        o = lax.rem(mine + i, 16)
        remote(send_a.at[o], recv_a.at[mine], 4, peer(o)).start()
        return carry

    lax.fori_loop(1, 16, send_plane, 0)
    recv_a[mine] = send_a[mine]
    lax.fori_loop(0, 32, functools.partial(send_grad, 1), 0)
    all_of(send_a, recv_a, 4, 15).wait_recv()
    total = recv_a[0]
    for o in range(1, 16):
        total = total + recv_a[o]
    send_b[...] = total

    def send_z(i, carry):
        o = lax.rem(z + i, 4)
        remote(send_b.at[o], recv_b.at[z], 5, (e, me + (o - z) * 4)).start()
        return carry

    lax.fori_loop(1, 4, send_z, 0)
    recv_b[z] = send_b[z]
    lax.fori_loop(32, 64, functools.partial(send_grad, 1), 0)
    all_of(send_b, recv_b, 5, 3).wait_recv()
    total = recv_b[0] + recv_b[1] + recv_b[2] + recv_b[3]
    send_e[0] = total

    def send_ens(i, carry):
        remote(send_e.at[0], recv_e.at[e], 6, (lax.rem(e + i, 8), me)).start()
        return carry

    lax.fori_loop(1, 8, send_ens, 0)
    recv_e[e] = total
    recv_g1[me] = send_g1[me]

    all_of(send_g0, recv_g0, 7, 63).wait_recv()
    all_of(send_g1, recv_g1, 8, 63).wait_recv()
    for f in range(2):
        at = slice(32 * f, 32 * (f + 1))
        t = jnp.concatenate([recv_g0[at].astype(F32), recv_g1[at].astype(F32)], axis=2)
        for h in range(2):
            g = t[:, 8 * h : 8 * (h + 1), :].reshape(256, 384).astype(BF)
            branch = dot(lon_t[...], g)
            lanes = slice(384 * f, 384 * (f + 1))
            out[h, :, lanes] = (cot[h, :, lanes].astype(F32) + branch).astype(BF)

    all_of(recv_e, recv_e, 6, 7).wait_recv()
    out_w[:8, :] = recv_e[0] + recv_e[2] + recv_e[4] + recv_e[6]
    total = recv_e[1] + recv_e[3] + recv_e[5] + recv_e[7]
    hi, lo = halves(jnp.broadcast_to(total[4:5], (8, 384)))
    lane, to = iota((384, 384), 0), iota((384, 384), 1)
    line = iota((8, 384), 0)
    for part in range(4):
        at = 96 * part + lax.rem(me, 8) * 12
        choose = jnp.where((lane == to + at) & (to < 12), 1.0, 0.0).astype(BF)
        total = jnp.where(line == 4 + part, dot(hi, choose) + dot(lo, choose), total)
    out_w[8:, :] = total

    all_of(send_t, recv_t, 0, 63).wait_send()
    all_of(send_s, recv_s, 1, 63).wait_send()
    all_of(send_cx, recv_cx, 2, 63).wait_send()
    all_of(send_cy, recv_cy, 3, 63).wait_send()
    all_of(send_g0, recv_g0, 7, 63).wait_send()
    all_of(send_g1, recv_g1, 8, 63).wait_send()
    all_of(send_a, recv_a, 4, 15).wait_send()
    all_of(send_b, recv_b, 5, 3).wait_send()
    all_of(recv_e, recv_e, 6, 7).wait_send()


def shards(tables, tokens, cotangent, w_first, b_first, w_second, b_second):
    blocks = lambda n, kind: pltpu.VMEM((n, 16, 384), kind)
    parts = lambda kind: pltpu.VMEM((4, 256, 384), kind)
    loaded = [(2, 384, 768), (2, 384, 768), (192, 768), (2, 768), (192, 768), (2, 768)]
    scratch = [pltpu.VMEM(n, BF) for n in loaded] + [pltpu.VMEM(t.shape, BF) for t in tables]
    scratch += [
        pltpu.SemaphoreType.DMA((13,)),
        pltpu.VMEM((2, 2, 256, 384), F32),
        blocks(64, BF), pltpu.VMEM((64, 1, 128), F32), blocks(64, BF), pltpu.VMEM((64, 1, 128), F32),
        pltpu.VMEM((64, 16, 256), BF), pltpu.VMEM((64, 16, 256), BF), pltpu.VMEM((64, 16, 128), BF), pltpu.VMEM((64, 16, 128), BF),
        pltpu.VMEM((64, 16, 128), BF), pltpu.VMEM((64, 16, 128), BF), pltpu.VMEM((64, 16, 256), BF), pltpu.VMEM((64, 16, 256), BF),
        pltpu.VMEM((4, 256, 128), F32),
        pltpu.VMEM((3, 1024, 128), F32),
        parts(BF), parts(BF), parts(BF), parts(BF),
        pltpu.VMEM((1024, 384), BF), pltpu.VMEM((1024, 384), BF),
        pltpu.VMEM((384, 768), BF), pltpu.VMEM((384, 768), BF),
        pltpu.VMEM((4, 512, 256), BF), pltpu.VMEM((4, 512, 256), BF), pltpu.VMEM((4, 4, 256, 384), BF),
        pltpu.VMEM((16, 4, 8, 384), F32), pltpu.VMEM((16, 4, 8, 384), F32),
        pltpu.VMEM((4, 8, 384), F32), pltpu.VMEM((4, 8, 384), F32),
        pltpu.VMEM((1, 8, 384), F32), pltpu.VMEM((8, 8, 384), F32),
        pltpu.SemaphoreType.DMA((9,)), pltpu.SemaphoreType.DMA((9,)),
    ]
    spec = pl.BlockSpec(memory_space=pltpu.VMEM)
    field, grads = pl.pallas_call(
        kernel,
        out_shape=(jax.ShapeDtypeStruct((2, 384, 768), BF), jax.ShapeDtypeStruct((16, 384), F32)),
        in_specs=[pl.BlockSpec(memory_space=pl.ANY)] * 13,
        out_specs=(spec, spec),
        scratch_shapes=scratch,
        name="afno_backward",
        compiler_params=pltpu.CompilerParams(
            collective_id=0, has_side_effects=True, vmem_limit_bytes=60 << 20
        ),
    )(tokens[0], cotangent[0], w_first.T, b_first, w_second.T, b_second, *[jnp.asarray(t) for t in tables])
    return field[None], grads[:12, :192], grads[12:14, :12], grads[:12, 192:], grads[14:, :12]


def solution(mesh):
    return jax.shard_map(
        functools.partial(shards, constants()),
        mesh=mesh,
        in_specs=(P("ens", "sp", None, None), P("ens", "sp", None, None), P(), P(), P(), P()),
        out_specs=(
            P("ens", "sp", None, None),
            P("sp", None),
            P(None, "sp"),
            P("sp", None),
            P(None, "sp"),
        ),
        check_vma=False,
    )
```

```python
import functools

import jax
import jax.numpy as jnp
import ml_dtypes
import numpy as np
from jax import lax
from jax.experimental import pallas as pl
from jax.experimental.pallas import tpu as pltpu
from jax.sharding import PartitionSpec as P

MESH = pl.DeviceIdType.MESH
BF = jnp.bfloat16
F32 = jnp.float32
LEVEL = 0.01
CODE_SPAN = 249.0
CODE_BASE = 124.0
FACTOR = float(131072) ** (-0.5)
WINDOWS = (0, 0, 128, 128)


def constants():
    k = np.arange(128)[:, None]
    w = np.arange(384)[None, :]
    a = 2.0 * np.pi * ((k * w) % 384) / 384.0
    lon = (np.stack([np.cos(a), -np.sin(a)]) / np.sqrt(384.0)).astype(np.float32)
    lon = lon.reshape(2, 32, 4, 384).transpose(1, 0, 2, 3).reshape(256, 384)
    m = np.arange(128)[:, None]
    h = np.arange(128)[None, :]
    b = 2.0 * np.pi * ((m * h) % 128) / 128.0
    c, s = np.cos(b) / np.sqrt(128.0), np.sin(b) / np.sqrt(128.0)
    lat = np.stack([np.stack([c, s], 2), np.stack([-s, c], 2)])
    lat = lat.astype(np.float32).reshape(256, 256)

    def split(t):
        hi = t.astype(ml_dtypes.bfloat16)
        return hi, (t - hi.astype(np.float32)).astype(ml_dtypes.bfloat16)

    lon_hi, lon_lo = split(lon)
    lat_hi, lat_lo = split(lat)
    place = np.zeros((2, 2, 4, 2, 16, 384), np.float32)
    for yy in range(2):
        for z in range(4):
            for x in range(4):
                for r in range(12):
                    place[yy, z // 2, x, z % 2, r, yy * 192 + z * 48 + x * 12 + r] = 1.0
    place = place.reshape(512, 384).astype(ml_dtypes.bfloat16)
    return [lon_hi, lon_lo, lat_hi, lat_lo, np.ascontiguousarray(lat_hi.T), place], np.ascontiguousarray(lon_hi.T)


def dot(a, b):
    return lax.dot_general(a, b, (((1,), (0,)), ((), ())), preferred_element_type=F32)


def dot_t(a, b):
    return lax.dot_general(a, b, (((1,), (1,)), ((), ())), preferred_element_type=F32)


def halves(x):
    hi = x.astype(BF)
    return hi, (x - hi.astype(F32)).astype(BF)


def iota(shape, dim):
    return lax.broadcasted_iota(jnp.int32, shape, dim)


def block_of(i):
    return (i >= 96).astype(jnp.int32) + (i >= 192).astype(jnp.int32) + (i >= 288).astype(jnp.int32)


def wide(s):
    return jnp.concatenate([s, s, s], axis=1)


def kernel(
    tok_a, cot_a, w1_a, b1_a, w2_a, b2_a, lon_hi_a, lon_lo_a, lat_hi_a, lat_lo_a, lat_t_a, place_a,
    recv_g0, recv_g1, out_w,
    tok, cot, w1, b1, w2, b2, lon_hi, lon_lo, lat_hi, lat_lo, lat_t, place, load,
    lonbuf, send_t, send_s, recv_t, recv_s, send_cx, recv_cx, send_cy, recv_cy, send_g0, send_g1, middle,
    rows, xh, xl, first_b, mask_b, g1_b, g2_b, v1, v2, left1, left2, pick,
    send_a, recv_a, send_b, recv_b, send_e, recv_e, ss, rs,
):
    pairs = [
        (lon_hi_a, lon_hi), (lon_lo_a, lon_lo), (tok_a, tok), (cot_a, cot), (w1_a, w1), (b1_a, b1), (w2_a, w2),
        (b2_a, b2), (lat_hi_a, lat_hi), (lat_lo_a, lat_lo), (lat_t_a, lat_t), (place_a, place),
    ]
    loads = [pltpu.make_async_copy(a, b, load.at[n]) for n, (a, b) in enumerate(pairs)]
    for copy in loads:
        copy.start()
    e = lax.axis_index("ens")
    me = lax.axis_index("sp")
    half = lax.div(me, 32)
    barrier = pltpu.get_barrier_semaphore()

    def greet(i, carry):
        pl.semaphore_signal(barrier, inc=1, device_id=(e, lax.rem(me + i, 64)), device_id_type=MESH)
        return carry

    def greet_ens(i, carry):
        pl.semaphore_signal(barrier, inc=1, device_id=(lax.rem(e + i, 8), me), device_id_type=MESH)
        return carry

    lax.fori_loop(1, 64, greet, 0)
    lax.fori_loop(1, 8, greet_ens, 0)
    x = lax.rem(me, 4)
    y = lax.div(me, 16)
    z = lax.rem(lax.div(me, 4), 4)
    core = lax.rem(e, 2)
    mine = core * 8 + lax.rem(y, 2) * 4 + x

    def peer(o):
        j = lax.rem(o, 8)
        return (e - core + lax.div(o, 8), half * 32 + lax.div(j, 4) * 16 + z * 4 + lax.rem(j, 4))

    def greet_core(i, carry):
        o = (1 - core) * 8 + lax.rem(mine + i, 8)
        pl.semaphore_signal(barrier, inc=1, device_id=peer(o), device_id_type=MESH)
        return carry

    lax.fori_loop(1, 8, greet_core, 0)

    def remote(src, dst, j, dev):
        return pltpu.make_async_remote_copy(
            src, dst, ss.at[j], rs.at[j], device_id=dev, device_id_type=MESH
        )

    def all_of(src, dst, j, n):
        return remote(src.at[pl.ds(0, n)], dst.at[pl.ds(0, n)], j, (e, lax.rem(me + 1, 64)))

    for copy in loads[:3]:
        copy.wait()
    for h in range(2):
        for f in range(2):
            t = tok[h, :, f * 384 : (f + 1) * 384]
            lonbuf[f, h] = dot(lon_hi[...], t) + dot(lon_lo[...], t)
    pl.semaphore_wait(barrier, 77)

    def dest(i):
        return lax.rem(me + i, 64)

    def pair(buf, d):
        f, g = lax.div(d, 32), pl.multiple_of(lax.rem(d, 32) * 8, 8)
        return jnp.concatenate([buf[f, 0, pl.ds(g, 8), :], buf[f, 1, pl.ds(g, 8), :]], axis=0)

    def send_tok(i, carry):
        d = dest(i)
        v = pair(lonbuf, d)
        av = jnp.abs(v)
        top = jnp.max(av, axis=0, keepdims=True)
        top = jnp.maximum(jnp.maximum(top[:, :128], top[:, 128:256]), top[:, 256:])
        top = jnp.maximum(top, 1e-30)
        coded = jnp.exp2(av * wide(CODE_SPAN / top) - CODE_BASE)
        send_t[d] = jnp.where(v < 0.0, -coded, coded).astype(BF)
        send_s[d] = top

        @pl.when(d != me)
        def _():
            remote(send_t.at[d], recv_t.at[me], 0, (e, d)).start()
            remote(send_s.at[d], recv_s.at[me], 1, (e, d)).start()

        return carry

    def send_cot(part, i, carry):
        d = dest(i)
        src, dst = (send_cx, recv_cx) if part == 0 else (send_cy, recv_cy)
        v = pair(lonbuf, d)
        src[d] = (v[:, :256] if part == 0 else v[:, 256:]).astype(BF)

        @pl.when(d != me)
        def _():
            remote(src.at[d], dst.at[me], 2 + part, (e, d)).start()

        return carry

    lax.fori_loop(0, 64, send_tok, 0)
    recv_t[me] = send_t[me]
    recv_s[me] = send_s[me]
    loads[3].wait()
    row = iota((256, 384), 0)
    scale = jnp.where((row == 0) | (row == 4), 1.0, 2.0)
    for h in range(2):
        for g in range(2):
            lonbuf[g, h] = dot(lon_hi[...], cot[h, :, g * 384 : (g + 1) * 384]) * scale
    lax.fori_loop(0, 64, functools.partial(send_cot, 0), 0)
    lax.fori_loop(0, 64, functools.partial(send_cot, 1), 0)
    recv_cx[me] = send_cx[me]
    recv_cy[me] = send_cy[me]

    for copy in loads[4:]:
        copy.wait()
    q, j = iota((192, 768), 0), iota((192, 768), 1)
    jm = jnp.where(j >= 384, j - 384, j)
    inner = jm - 96 * block_of(jm) + jnp.where(j >= 384, 96, 0)
    spread = jnp.where(q == inner, 1.0, 0.0).astype(BF)
    r, j = iota((384, 768), 0), iota((384, 768), 1)
    own = block_of(r) == block_of(jnp.where(j >= 384, j - 384, j))

    def diagonal(w):
        t = jnp.where(half == 0, w[:, :384].astype(F32), w[:, 384:].astype(F32)).astype(BF)
        t = lax.dot_general(t, spread, (((0,), (0,)), ((), ())), preferred_element_type=F32)
        return jnp.where(own, t, 0.0).astype(BF)

    v1[...] = diagonal(w1)
    v2[...] = diagonal(w2)

    def bias(ref):
        t = ref[...].astype(F32)
        t = jnp.where(half == 0, t[:, :384], t[:, 384:])
        return t[0:1], t[1:2]

    lane, to = iota((256, 384), 0), iota((256, 384), 1)
    for n in range(4):
        for part in range(4):
            at = 96 * n - WINDOWS[n]
            inside = (lane >= at) & (lane < at + 96)
            pick[n, part] = jnp.where((lane - at == to - 96 * part) & inside, 1.0, 0.0).astype(BF)
    slot, col = iota((512, 256), 0), iota((512, 256), 1)
    ones = jnp.where((jnp.bitwise_and(slot, 15) == 12) & (col < 128), 1.0, 0.0)

    b1r, b1i = bias(b1)
    b2r, b2i = bias(b2)

    all_of(send_t, recv_t, 0, 63).wait_recv()
    all_of(send_s, recv_s, 1, 63).wait_recv()

    def put_rows(i, x):
        for t in range(3):
            rows[t, pl.ds(pl.multiple_of(i * 16, 16), 16), :] = x[:, 128 * t : 128 * (t + 1)]

    def mode_rows(k):
        return jnp.concatenate([rows[t, pl.ds(k, 256, stride=4), :] for t in range(3)], axis=1)

    def decode(i, carry):
        y = recv_t[i].astype(F32)
        u = (jnp.log2(jnp.abs(y)) + CODE_BASE) * wide(recv_s[i] * (1.0 / CODE_SPAN))
        put_rows(i, jnp.where(y < 0.0, -u, u))
        return carry

    lax.fori_loop(0, 64, decode, 0, unroll=4)
    for k in range(4):
        hi, lo = halves(mode_rows(k))
        xh[k] = hi
        xl[k] = lo

    low = iota((256, 128), 1) < 64

    def join(a, b):
        return jnp.concatenate([a[:, :128], jnp.where(low, a[:, 128:], b[:, :128]), b[:, 128:]], axis=1)

    def mix(x, v, br, bi):
        hi, lo = halves(x)

        def window(w, col):
            here = slice(128 * w, 128 * w + 256)
            vw = v[here, 384 * col + 128 * w : 384 * col + 128 * w + 256]
            return dot(hi[:, here], vw) + dot(lo[:, here], vw)

        tr = join(window(0, 0), window(1, 0))
        ti = join(window(0, 1), window(1, 1))
        real = tr[:128] - ti[128:] + br
        imag = ti[:128] + tr[128:] + bi
        return hi, jnp.concatenate([real, imag], axis=0)

    def forward(k, carry):
        s = dot(lat_hi[...], xh[k]) + dot(lat_hi[...], xl[k]) + dot(lat_lo[...], xh[k])
        hi, pre = mix(s, v1, b1r, b1i)
        left1[k] = (dot_t(place[...], hi) + ones).astype(BF)
        hi, pre = mix(jnp.maximum(pre, 0.0), v2, b2r, b2i)
        first_b[k] = hi
        left2[k] = (dot_t(place[...], hi) + ones).astype(BF)
        mask_b[k] = jnp.where(jnp.abs(pre) > LEVEL, 1.0, 0.0).astype(BF)
        return carry

    lax.fori_loop(0, 4, forward, 0)

    def unpack(part, i, carry):
        at = pl.ds(pl.multiple_of(i * 16, 16), 16)
        if part == 0:
            t = recv_cx[i].astype(F32)
            rows[0, at, :] = t[:, :128]
            rows[1, at, :] = t[:, 128:]
        else:
            rows[2, at, :] = recv_cy[i].astype(F32)
        return carry

    def back(g, v, w):
        here = slice(128 * w, 128 * w + 256)
        br = dot_t(g, v[here, here])
        bi = dot_t(g, v[here, 384 + 128 * w : 640 + 128 * w])
        return jnp.concatenate([br[:128] + bi[128:], br[128:] - bi[:128]], axis=0)

    def backward(k, w):
        here = slice(128 * w, 128 * w + 256)
        mine = slice(256 * k, 256 * (k + 1))
        g2 = jnp.where(mask_b[k, :, here].astype(F32) > 0.0, dot(lat_hi[...], xh[k, :, here]), 0.0).astype(BF)
        g2_b[mine, here] = g2
        g1 = jnp.where(first_b[k, :, here].astype(F32) > 0.0, back(g2, v2, w), 0.0).astype(BF)
        if w == 0:
            g1_b[mine, here] = g1
        else:
            g1_b[mine, 128:256] = jnp.where(low, g1_b[mine, 128:256].astype(F32), g1[:, :128].astype(F32)).astype(BF)
            g1_b[mine, 256:] = g1[:, 128:]
        return dot(lat_t[...], back(g1, v1, w).astype(BF))

    def send_grad(part, i, carry):
        d = dest(i)
        at = pl.ds(pl.multiple_of(d * 16, 16), 16)
        src, dst = (send_g0, recv_g0) if part == 0 else (send_g1, recv_g1)
        if part == 0:
            src[d] = rows[0, at, :].astype(BF)
        else:
            src[d] = jnp.concatenate([rows[1, at, :], rows[2, at, :]], axis=1).astype(BF)

        @pl.when(d != me)
        def _():
            remote(src.at[d], dst.at[me], 7 + part, (e, d)).start()

        return carry

    all_of(send_cx, recv_cx, 2, 63).wait_recv()
    lax.fori_loop(0, 64, functools.partial(unpack, 0), 0, unroll=4)
    for k in range(4):
        for t in range(2):
            xh[k, :, 128 * t : 128 * (t + 1)] = rows[t, pl.ds(k, 256, stride=4), :].astype(BF)
    for k in range(4):
        g = backward(k, 0)
        rows[0, pl.ds(k, 256, stride=4), :] = g[:, :128]
        middle[k] = g[:, 128:]
    lax.fori_loop(0, 64, functools.partial(send_grad, 0), 0)
    own0 = pltpu.make_async_copy(send_g0.at[me], recv_g0.at[me], load.at[12])
    own0.start()

    all_of(send_cy, recv_cy, 3, 63).wait_recv()
    lax.fori_loop(0, 64, functools.partial(unpack, 1), 0, unroll=4)
    for k in range(4):
        xh[k, :, 256:] = rows[2, pl.ds(k, 256, stride=4), :].astype(BF)
    for k in range(4):
        g = backward(k, 1)
        rows[1, pl.ds(k, 256, stride=4), :] = jnp.where(low, middle[k], g[:, :128])
        rows[2, pl.ds(k, 256, stride=4), :] = g[:, 128:]

    def outer(n, left, g):
        lanes = slice(WINDOWS[n], WINDOWS[n] + 256)
        real, imag = 0.0, 0.0
        for k in range(4):
            lt = left[k, 128 * n : 128 * (n + 1), :]
            gr, gi = g[256 * k : 256 * k + 128, lanes], g[256 * k + 128 : 256 * (k + 1), lanes]
            real = real + dot(lt, jnp.concatenate([gr, gi], axis=0))
            imag = imag + dot(lt, jnp.concatenate([gi, -gr], axis=0))
        return real, imag

    for n in range(4):
        total = 0.0
        for part, t in enumerate(outer(n, left1, g1_b) + outer(n, left2, g2_b)):
            hi, lo = halves(t)
            total = total + dot(hi, pick[n, part]) + dot(lo, pick[n, part])
        total = (total * FACTOR).reshape(4, 2, 2, 8, 384)
        for zl in range(2):
            for c in range(2):
                at = c * 8 + 4 * (n // 2)
                send_a[at : at + 4, 2 * (n % 2) + zl] = total[:, zl, c]

    def send_plane(i, carry):
        o = lax.rem(mine + i, 16)
        remote(send_a.at[o], recv_a.at[mine], 4, peer(o)).start()
        return carry

    lax.fori_loop(1, 16, send_plane, 0)
    recv_a[mine] = send_a[mine]
    lax.fori_loop(0, 32, functools.partial(send_grad, 1), 0)
    all_of(send_a, recv_a, 4, 15).wait_recv()
    total = recv_a[0]
    for o in range(1, 16):
        total = total + recv_a[o]
    send_b[...] = total

    def send_z(i, carry):
        o = lax.rem(z + i, 4)
        remote(send_b.at[o], recv_b.at[z], 5, (e, me + (o - z) * 4)).start()
        return carry

    lax.fori_loop(1, 4, send_z, 0)
    recv_b[z] = send_b[z]
    lax.fori_loop(32, 64, functools.partial(send_grad, 1), 0)
    all_of(send_b, recv_b, 5, 3).wait_recv()
    total = recv_b[0] + recv_b[1] + recv_b[2] + recv_b[3]
    send_e[0] = total

    def send_ens(i, carry):
        remote(send_e.at[0], recv_e.at[e], 6, (lax.rem(e + i, 8), me)).start()
        return carry

    lax.fori_loop(1, 8, send_ens, 0)
    recv_e[e] = total
    own1 = pltpu.make_async_copy(send_g1.at[me], recv_g1.at[me], load.at[13])
    own1.start()

    all_of(recv_e, recv_e, 6, 7).wait_recv()
    out_w[:8, :] = recv_e[0] + recv_e[2] + recv_e[4] + recv_e[6]
    total = recv_e[1] + recv_e[3] + recv_e[5] + recv_e[7]
    hi, lo = halves(jnp.broadcast_to(total[4:5], (8, 384)))
    lane, to = iota((384, 384), 0), iota((384, 384), 1)
    line = iota((8, 384), 0)
    for part in range(4):
        at = 96 * part + lax.rem(me, 8) * 12
        choose = jnp.where((lane == to + at) & (to < 12), 1.0, 0.0).astype(BF)
        total = jnp.where(line == 4 + part, dot(hi, choose) + dot(lo, choose), total)
    out_w[8:, :] = total

    own0.wait()
    own1.wait()
    all_of(send_g0, recv_g0, 7, 63).wait_recv()
    all_of(send_g1, recv_g1, 8, 63).wait_recv()
    all_of(send_t, recv_t, 0, 63).wait_send()
    all_of(send_s, recv_s, 1, 63).wait_send()
    all_of(send_cx, recv_cx, 2, 63).wait_send()
    all_of(send_cy, recv_cy, 3, 63).wait_send()
    all_of(send_g0, recv_g0, 7, 63).wait_send()
    all_of(send_g1, recv_g1, 8, 63).wait_send()
    all_of(send_a, recv_a, 4, 15).wait_send()
    all_of(send_b, recv_b, 5, 3).wait_send()
    all_of(recv_e, recv_e, 6, 7).wait_send()


def finish(cot, first, second, sums, lon_t, out, w1, b1, w2, b2):
    t = jnp.concatenate([first[...].astype(F32), second[...].astype(F32)], axis=2)
    for h in range(2):
        g = t[:, 8 * h : 8 * (h + 1), :].reshape(256, 384).astype(BF)
        out[h] = (cot[h].astype(F32) + dot(lon_t[...], g)).astype(BF)
    w1[...] = sums[:12, :192]
    w2[...] = sums[:12, 192:]
    b1[...] = sums[12:14, :12]
    b2[...] = sums[14:, :12]


def shards(tables, lon_t, tokens, cotangent, w_first, b_first, w_second, b_second):
    blocks = lambda n, kind: pltpu.VMEM((n, 16, 384), kind)
    parts = lambda kind: pltpu.VMEM((4, 256, 384), kind)
    loaded = [(2, 384, 768), (2, 384, 768), (192, 768), (2, 768), (192, 768), (2, 768)]
    scratch = [pltpu.VMEM(n, BF) for n in loaded] + [pltpu.VMEM(t.shape, BF) for t in tables]
    scratch += [
        pltpu.SemaphoreType.DMA((14,)),
        pltpu.VMEM((2, 2, 256, 384), F32),
        blocks(64, BF), pltpu.VMEM((64, 1, 128), F32), blocks(64, BF), pltpu.VMEM((64, 1, 128), F32),
        pltpu.VMEM((64, 16, 256), BF), pltpu.VMEM((64, 16, 256), BF), pltpu.VMEM((64, 16, 128), BF), pltpu.VMEM((64, 16, 128), BF),
        pltpu.VMEM((64, 16, 128), BF), pltpu.VMEM((64, 16, 256), BF),
        pltpu.VMEM((4, 256, 128), F32),
        pltpu.VMEM((3, 1024, 128), F32),
        parts(BF), parts(BF), parts(BF), parts(BF),
        pltpu.VMEM((1024, 384), BF), pltpu.VMEM((1024, 384), BF),
        pltpu.VMEM((384, 768), BF), pltpu.VMEM((384, 768), BF),
        pltpu.VMEM((4, 512, 256), BF), pltpu.VMEM((4, 512, 256), BF), pltpu.VMEM((4, 4, 256, 384), BF),
        pltpu.VMEM((16, 4, 8, 384), F32), pltpu.VMEM((16, 4, 8, 384), F32),
        pltpu.VMEM((4, 8, 384), F32), pltpu.VMEM((4, 8, 384), F32),
        pltpu.VMEM((1, 8, 384), F32), pltpu.VMEM((8, 8, 384), F32),
        pltpu.SemaphoreType.DMA((9,)), pltpu.SemaphoreType.DMA((9,)),
    ]
    spec = pl.BlockSpec(memory_space=pl.ANY)
    first, second, sums = pl.pallas_call(
        kernel,
        out_shape=(
            jax.ShapeDtypeStruct((64, 16, 128), BF),
            jax.ShapeDtypeStruct((64, 16, 256), BF),
            jax.ShapeDtypeStruct((16, 384), F32),
        ),
        in_specs=[spec] * 12,
        out_specs=(spec, spec, pl.BlockSpec(memory_space=pltpu.VMEM)),
        scratch_shapes=scratch,
        name="afno_backward",
        compiler_params=pltpu.CompilerParams(
            collective_id=0, has_side_effects=True, vmem_limit_bytes=60 << 20
        ),
    )(tokens[0], cotangent[0], w_first.T, b_first, w_second.T, b_second, *[jnp.asarray(t) for t in tables])
    whole = lambda *shape: pl.BlockSpec(shape, lambda f: (0,) * len(shape))
    field = lambda: pl.BlockSpec((2, 384, 384), lambda f: (0, 0, f))
    part = lambda lanes: pl.BlockSpec((32, 16, lanes), lambda f: (f, 0, 0))
    out, w1, b1, w2, b2 = pl.pallas_call(
        finish,
        grid=(2,),
        out_shape=(
            jax.ShapeDtypeStruct((2, 384, 768), BF),
            jax.ShapeDtypeStruct((12, 192), F32),
            jax.ShapeDtypeStruct((2, 12), F32),
            jax.ShapeDtypeStruct((12, 192), F32),
            jax.ShapeDtypeStruct((2, 12), F32),
        ),
        in_specs=[field(), part(128), part(256), whole(16, 384), whole(384, 256)],
        out_specs=(field(), whole(12, 192), whole(2, 12), whole(12, 192), whole(2, 12)),
        name="finish",
        compiler_params=pltpu.CompilerParams(vmem_limit_bytes=60 << 20),
    )(cotangent[0], first, second, sums, jnp.asarray(lon_t))
    return out[None], w1, b1, w2, b2


def solution(mesh):
    return jax.shard_map(
        functools.partial(shards, *constants()),
        mesh=mesh,
        in_specs=(P("ens", "sp", None, None), P("ens", "sp", None, None), P(), P(), P(), P()),
        out_specs=(
            P("ens", "sp", None, None),
            P("sp", None),
            P(None, "sp"),
            P("sp", None),
            P(None, "sp"),
        ),
        check_vma=False,
    )
```

```python
import functools

import jax
import jax.numpy as jnp
import ml_dtypes
import numpy as np
from jax import lax
from jax.experimental import pallas as pl
from jax.experimental.pallas import tpu as pltpu
from jax.sharding import PartitionSpec as P

MESH = pl.DeviceIdType.MESH
BF = jnp.bfloat16
F32 = jnp.float32
LEVEL = 0.01
CODE_SPAN = 249.0
CODE_BASE = 124.0
FACTOR = float(131072) ** (-0.5)
WINDOWS = (0, 0, 128, 128)


def constants():
    k = np.arange(128)[:, None]
    w = np.arange(384)[None, :]
    a = 2.0 * np.pi * ((k * w) % 384) / 384.0
    lon = (np.stack([np.cos(a), -np.sin(a)]) / np.sqrt(384.0)).astype(np.float32)
    lon = lon.reshape(2, 32, 4, 384).transpose(1, 0, 2, 3).reshape(256, 384)
    m = np.arange(128)[:, None]
    h = np.arange(128)[None, :]
    b = 2.0 * np.pi * ((m * h) % 128) / 128.0
    c, s = np.cos(b) / np.sqrt(128.0), np.sin(b) / np.sqrt(128.0)
    lat = np.stack([np.stack([c, s], 2), np.stack([-s, c], 2)])
    lat = lat.astype(np.float32).reshape(256, 256)

    def split(t):
        hi = t.astype(ml_dtypes.bfloat16)
        return hi, (t - hi.astype(np.float32)).astype(ml_dtypes.bfloat16)

    lon_hi, lon_lo = split(lon)
    lat_hi, lat_lo = split(lat)
    place = np.zeros((2, 2, 4, 2, 16, 384), np.float32)
    for yy in range(2):
        for z in range(4):
            for x in range(4):
                for r in range(12):
                    place[yy, z // 2, x, z % 2, r, yy * 192 + z * 48 + x * 12 + r] = 1.0
    place = place.reshape(512, 384).astype(ml_dtypes.bfloat16)
    return [lon_hi, lon_lo, lat_hi, lat_lo, np.ascontiguousarray(lat_hi.T), place], np.ascontiguousarray(lon_hi.T)


def dot(a, b):
    return lax.dot_general(a, b, (((1,), (0,)), ((), ())), preferred_element_type=F32)


def dot_t(a, b):
    return lax.dot_general(a, b, (((1,), (1,)), ((), ())), preferred_element_type=F32)


def halves(x):
    hi = x.astype(BF)
    return hi, (x - hi.astype(F32)).astype(BF)


def iota(shape, dim):
    return lax.broadcasted_iota(jnp.int32, shape, dim)


def block_of(i):
    return (i >= 96).astype(jnp.int32) + (i >= 192).astype(jnp.int32) + (i >= 288).astype(jnp.int32)


def wide(s):
    return jnp.concatenate([s, s, s], axis=1)


def kernel(
    tok_a, cot_a, w1_a, b1_a, w2_a, b2_a, lon_hi_a, lon_lo_a, lat_hi_a, lat_lo_a, lat_t_a, place_a,
    recv_g0, recv_g1, out_w,
    tok, cot, w1, b1, w2, b2, lon_hi, lon_lo, lat_hi, lat_lo, lat_t, place, load,
    lonbuf, send_t, send_s, recv_t, recv_s, send_cx, recv_cx, send_cy, recv_cy, send_g0, send_g1, middle,
    rows, xh, xl, first_b, mask_b, g1_b, g2_b, v1, v2, left1, left2, pick,
    send_a, recv_a, send_b, recv_b, send_e, recv_e, ss, rs,
):
    pairs = [
        (lon_hi_a, lon_hi), (lon_lo_a, lon_lo), (tok_a, tok), (cot_a, cot), (w1_a, w1), (b1_a, b1), (w2_a, w2),
        (b2_a, b2), (lat_hi_a, lat_hi), (lat_lo_a, lat_lo), (lat_t_a, lat_t), (place_a, place),
    ]
    loads = [pltpu.make_async_copy(a, b, load.at[n]) for n, (a, b) in enumerate(pairs)]
    for copy in loads:
        copy.start()
    e = lax.axis_index("ens")
    me = lax.axis_index("sp")
    half = lax.div(me, 32)
    barrier = pltpu.get_barrier_semaphore()

    def greet(i, carry):
        pl.semaphore_signal(barrier, inc=1, device_id=(e, lax.rem(me + i, 64)), device_id_type=MESH)
        return carry

    def greet_ens(i, carry):
        pl.semaphore_signal(barrier, inc=1, device_id=(lax.rem(e + i, 8), me), device_id_type=MESH)
        return carry

    lax.fori_loop(1, 64, greet, 0)
    lax.fori_loop(1, 8, greet_ens, 0)
    x = lax.rem(me, 4)
    y = lax.div(me, 16)
    z = lax.rem(lax.div(me, 4), 4)
    core = lax.rem(e, 2)
    mine = core * 8 + lax.rem(y, 2) * 4 + x

    def peer(o):
        j = lax.rem(o, 8)
        return (e - core + lax.div(o, 8), half * 32 + lax.div(j, 4) * 16 + z * 4 + lax.rem(j, 4))

    def greet_core(i, carry):
        o = (1 - core) * 8 + lax.rem(mine + i, 8)
        pl.semaphore_signal(barrier, inc=1, device_id=peer(o), device_id_type=MESH)
        return carry

    lax.fori_loop(1, 8, greet_core, 0)

    def remote(src, dst, j, dev):
        return pltpu.make_async_remote_copy(
            src, dst, ss.at[j], rs.at[j], device_id=dev, device_id_type=MESH
        )

    def all_of(src, dst, j, n):
        return remote(src.at[pl.ds(0, n)], dst.at[pl.ds(0, n)], j, (e, lax.rem(me + 1, 64)))

    for copy in loads[:3]:
        copy.wait()
    for h in range(2):
        for f in range(2):
            t = tok[h, :, f * 384 : (f + 1) * 384]
            lonbuf[f, h] = dot(lon_hi[...], t) + dot(lon_lo[...], t)
    pl.semaphore_wait(barrier, 77)

    def dest(i):
        return lax.rem(me + i * (1 + 62 * core), 64)

    def pair(buf, d):
        f, g = lax.div(d, 32), pl.multiple_of(lax.rem(d, 32) * 8, 8)
        return jnp.concatenate([buf[f, 0, pl.ds(g, 8), :], buf[f, 1, pl.ds(g, 8), :]], axis=0)

    def send_tok(i, carry):
        d = dest(i)
        v = pair(lonbuf, d)
        av = jnp.abs(v)
        top = jnp.max(av, axis=0, keepdims=True)
        top = jnp.maximum(jnp.maximum(top[:, :128], top[:, 128:256]), top[:, 256:])
        top = jnp.maximum(top, 1e-30)
        coded = jnp.exp2(av * wide(CODE_SPAN / top) - CODE_BASE)
        send_t[d] = jnp.where(v < 0.0, -coded, coded).astype(BF)
        send_s[d] = top

        @pl.when(d != me)
        def _():
            remote(send_t.at[d], recv_t.at[me], 0, (e, d)).start()
            remote(send_s.at[d], recv_s.at[me], 1, (e, d)).start()

        return carry

    def send_cot(part, i, carry):
        d = dest(i)
        src, dst = (send_cx, recv_cx) if part == 0 else (send_cy, recv_cy)
        v = pair(lonbuf, d)
        src[d] = (v[:, :256] if part == 0 else v[:, 256:]).astype(BF)

        @pl.when(d != me)
        def _():
            remote(src.at[d], dst.at[me], 2 + part, (e, d)).start()

        return carry

    lax.fori_loop(0, 64, send_tok, 0)
    recv_t[me] = send_t[me]
    recv_s[me] = send_s[me]
    loads[3].wait()
    row = iota((256, 384), 0)
    scale = jnp.where((row == 0) | (row == 4), 1.0, 2.0)
    for h in range(2):
        for g in range(2):
            lonbuf[g, h] = dot(lon_hi[...], cot[h, :, g * 384 : (g + 1) * 384]) * scale
    lax.fori_loop(0, 64, functools.partial(send_cot, 0), 0)
    lax.fori_loop(0, 64, functools.partial(send_cot, 1), 0)
    recv_cx[me] = send_cx[me]
    recv_cy[me] = send_cy[me]

    for copy in loads[4:]:
        copy.wait()
    q, j = iota((192, 768), 0), iota((192, 768), 1)
    jm = jnp.where(j >= 384, j - 384, j)
    inner = jm - 96 * block_of(jm) + jnp.where(j >= 384, 96, 0)
    spread = jnp.where(q == inner, 1.0, 0.0).astype(BF)
    r, j = iota((384, 768), 0), iota((384, 768), 1)
    own = block_of(r) == block_of(jnp.where(j >= 384, j - 384, j))

    def diagonal(w):
        t = jnp.where(half == 0, w[:, :384].astype(F32), w[:, 384:].astype(F32)).astype(BF)
        t = lax.dot_general(t, spread, (((0,), (0,)), ((), ())), preferred_element_type=F32)
        return jnp.where(own, t, 0.0).astype(BF)

    v1[...] = diagonal(w1)
    v2[...] = diagonal(w2)

    def bias(ref):
        t = ref[...].astype(F32)
        t = jnp.where(half == 0, t[:, :384], t[:, 384:])
        return t[0:1], t[1:2]

    lane, to = iota((256, 384), 0), iota((256, 384), 1)
    for n in range(4):
        for part in range(4):
            at = 96 * n - WINDOWS[n]
            inside = (lane >= at) & (lane < at + 96)
            pick[n, part] = jnp.where((lane - at == to - 96 * part) & inside, 1.0, 0.0).astype(BF)
    slot, col = iota((512, 256), 0), iota((512, 256), 1)
    ones = jnp.where((jnp.bitwise_and(slot, 15) == 12) & (col < 128), 1.0, 0.0)

    b1r, b1i = bias(b1)
    b2r, b2i = bias(b2)

    all_of(send_t, recv_t, 0, 63).wait_recv()
    all_of(send_s, recv_s, 1, 63).wait_recv()

    def put_rows(i, x):
        for t in range(3):
            rows[t, pl.ds(pl.multiple_of(i * 16, 16), 16), :] = x[:, 128 * t : 128 * (t + 1)]

    def mode_rows(k):
        return jnp.concatenate([rows[t, pl.ds(k, 256, stride=4), :] for t in range(3)], axis=1)

    def decode(i, carry):
        y = recv_t[i].astype(F32)
        u = (jnp.log2(jnp.abs(y)) + CODE_BASE) * wide(recv_s[i] * (1.0 / CODE_SPAN))
        put_rows(i, jnp.where(y < 0.0, -u, u))
        return carry

    lax.fori_loop(0, 64, decode, 0, unroll=4)
    for k in range(4):
        hi, lo = halves(mode_rows(k))
        xh[k] = hi
        xl[k] = lo

    low = iota((256, 128), 1) < 64

    def join(a, b):
        return jnp.concatenate([a[:, :128], jnp.where(low, a[:, 128:], b[:, :128]), b[:, 128:]], axis=1)

    def mix(x, v, br, bi):
        hi, lo = halves(x)

        def window(w, col):
            here = slice(128 * w, 128 * w + 256)
            vw = v[here, 384 * col + 128 * w : 384 * col + 128 * w + 256]
            return dot(hi[:, here], vw) + dot(lo[:, here], vw)

        tr = join(window(0, 0), window(1, 0))
        ti = join(window(0, 1), window(1, 1))
        real = tr[:128] - ti[128:] + br
        imag = ti[:128] + tr[128:] + bi
        return hi, jnp.concatenate([real, imag], axis=0)

    def forward(k, carry):
        s = dot(lat_hi[...], xh[k]) + dot(lat_hi[...], xl[k]) + dot(lat_lo[...], xh[k])
        hi, pre = mix(s, v1, b1r, b1i)
        left1[k] = (dot_t(place[...], hi) + ones).astype(BF)
        hi, pre = mix(jnp.maximum(pre, 0.0), v2, b2r, b2i)
        first_b[k] = hi
        left2[k] = (dot_t(place[...], hi) + ones).astype(BF)
        mask_b[k] = jnp.where(jnp.abs(pre) > LEVEL, 1.0, 0.0).astype(BF)
        return carry

    lax.fori_loop(0, 4, forward, 0)

    def unpack(part, i, carry):
        at = pl.ds(pl.multiple_of(i * 16, 16), 16)
        if part == 0:
            t = recv_cx[i].astype(F32)
            rows[0, at, :] = t[:, :128]
            rows[1, at, :] = t[:, 128:]
        else:
            rows[2, at, :] = recv_cy[i].astype(F32)
        return carry

    def back(g, v, w):
        here = slice(128 * w, 128 * w + 256)
        br = dot_t(g, v[here, here])
        bi = dot_t(g, v[here, 384 + 128 * w : 640 + 128 * w])
        return jnp.concatenate([br[:128] + bi[128:], br[128:] - bi[:128]], axis=0)

    def backward(k, w):
        here = slice(128 * w, 128 * w + 256)
        mine = slice(256 * k, 256 * (k + 1))
        g2 = jnp.where(mask_b[k, :, here].astype(F32) > 0.0, dot(lat_hi[...], xh[k, :, here]), 0.0).astype(BF)
        g2_b[mine, here] = g2
        g1 = jnp.where(first_b[k, :, here].astype(F32) > 0.0, back(g2, v2, w), 0.0).astype(BF)
        if w == 0:
            g1_b[mine, here] = g1
        else:
            g1_b[mine, 128:256] = jnp.where(low, g1_b[mine, 128:256].astype(F32), g1[:, :128].astype(F32)).astype(BF)
            g1_b[mine, 256:] = g1[:, 128:]
        return dot(lat_t[...], back(g1, v1, w).astype(BF))

    def send_grad(part, i, carry):
        d = dest(i)
        at = pl.ds(pl.multiple_of(d * 16, 16), 16)
        src, dst = (send_g0, recv_g0) if part == 0 else (send_g1, recv_g1)
        if part == 0:
            src[d] = rows[0, at, :].astype(BF)
        else:
            src[d] = jnp.concatenate([rows[1, at, :], rows[2, at, :]], axis=1).astype(BF)

        @pl.when(d != me)
        def _():
            remote(src.at[d], dst.at[me], 7 + part, (e, d)).start()

        return carry

    all_of(send_cx, recv_cx, 2, 63).wait_recv()
    lax.fori_loop(0, 64, functools.partial(unpack, 0), 0, unroll=4)
    for k in range(4):
        for t in range(2):
            xh[k, :, 128 * t : 128 * (t + 1)] = rows[t, pl.ds(k, 256, stride=4), :].astype(BF)
    for k in range(4):
        g = backward(k, 0)
        rows[0, pl.ds(k, 256, stride=4), :] = g[:, :128]
        middle[k] = g[:, 128:]
    lax.fori_loop(0, 64, functools.partial(send_grad, 0), 0)
    own0 = pltpu.make_async_copy(send_g0.at[me], recv_g0.at[me], load.at[12])
    own0.start()

    all_of(send_cy, recv_cy, 3, 63).wait_recv()
    lax.fori_loop(0, 64, functools.partial(unpack, 1), 0, unroll=4)
    for k in range(4):
        xh[k, :, 256:] = rows[2, pl.ds(k, 256, stride=4), :].astype(BF)
    for k in range(4):
        g = backward(k, 1)
        rows[1, pl.ds(k, 256, stride=4), :] = jnp.where(low, middle[k], g[:, :128])
        rows[2, pl.ds(k, 256, stride=4), :] = g[:, 128:]

    def outer(n, left, g):
        lanes = slice(WINDOWS[n], WINDOWS[n] + 256)
        real, imag = 0.0, 0.0
        for k in range(4):
            lt = left[k, 128 * n : 128 * (n + 1), :]
            gr, gi = g[256 * k : 256 * k + 128, lanes], g[256 * k + 128 : 256 * (k + 1), lanes]
            real = real + dot(lt, jnp.concatenate([gr, gi], axis=0))
            imag = imag + dot(lt, jnp.concatenate([gi, -gr], axis=0))
        return real, imag

    for n in range(4):
        total = 0.0
        for part, t in enumerate(outer(n, left1, g1_b) + outer(n, left2, g2_b)):
            hi, lo = halves(t)
            total = total + dot(hi, pick[n, part]) + dot(lo, pick[n, part])
        total = (total * FACTOR).reshape(4, 2, 2, 8, 384)
        for zl in range(2):
            for c in range(2):
                at = c * 8 + 4 * (n // 2)
                send_a[at : at + 4, 2 * (n % 2) + zl] = total[:, zl, c]

    def send_plane(i, carry):
        o = lax.rem(mine + i, 16)
        remote(send_a.at[o], recv_a.at[mine], 4, peer(o)).start()
        return carry

    lax.fori_loop(1, 16, send_plane, 0)
    recv_a[mine] = send_a[mine]
    lax.fori_loop(0, 32, functools.partial(send_grad, 1), 0)
    all_of(send_a, recv_a, 4, 15).wait_recv()
    total = recv_a[0]
    for o in range(1, 16):
        total = total + recv_a[o]
    send_b[...] = total

    def send_z(i, carry):
        o = lax.rem(z + i, 4)
        remote(send_b.at[o], recv_b.at[z], 5, (e, me + (o - z) * 4)).start()
        return carry

    lax.fori_loop(1, 4, send_z, 0)
    recv_b[z] = send_b[z]
    lax.fori_loop(32, 64, functools.partial(send_grad, 1), 0)
    all_of(send_b, recv_b, 5, 3).wait_recv()
    total = recv_b[0] + recv_b[1] + recv_b[2] + recv_b[3]
    send_e[0] = total

    def send_ens(i, carry):
        remote(send_e.at[0], recv_e.at[e], 6, (lax.rem(e + i, 8), me)).start()
        return carry

    lax.fori_loop(1, 8, send_ens, 0)
    recv_e[e] = total
    own1 = pltpu.make_async_copy(send_g1.at[me], recv_g1.at[me], load.at[13])
    own1.start()

    all_of(recv_e, recv_e, 6, 7).wait_recv()
    out_w[:8, :] = recv_e[0] + recv_e[2] + recv_e[4] + recv_e[6]
    total = recv_e[1] + recv_e[3] + recv_e[5] + recv_e[7]
    hi, lo = halves(jnp.broadcast_to(total[4:5], (8, 384)))
    lane, to = iota((384, 384), 0), iota((384, 384), 1)
    line = iota((8, 384), 0)
    for part in range(4):
        at = 96 * part + lax.rem(me, 8) * 12
        choose = jnp.where((lane == to + at) & (to < 12), 1.0, 0.0).astype(BF)
        total = jnp.where(line == 4 + part, dot(hi, choose) + dot(lo, choose), total)
    out_w[8:, :] = total

    own0.wait()
    own1.wait()
    all_of(send_g0, recv_g0, 7, 63).wait_recv()
    all_of(send_g1, recv_g1, 8, 63).wait_recv()
    all_of(send_t, recv_t, 0, 63).wait_send()
    all_of(send_s, recv_s, 1, 63).wait_send()
    all_of(send_cx, recv_cx, 2, 63).wait_send()
    all_of(send_cy, recv_cy, 3, 63).wait_send()
    all_of(send_g0, recv_g0, 7, 63).wait_send()
    all_of(send_g1, recv_g1, 8, 63).wait_send()
    all_of(send_a, recv_a, 4, 15).wait_send()
    all_of(send_b, recv_b, 5, 3).wait_send()
    all_of(recv_e, recv_e, 6, 7).wait_send()


def finish(cot, first, second, sums, lon_t, out, w1, b1, w2, b2):
    t = jnp.concatenate([first[...].astype(F32), second[...].astype(F32)], axis=2)
    for h in range(2):
        g = t[:, 8 * h : 8 * (h + 1), :].reshape(256, 384).astype(BF)
        out[h] = (cot[h].astype(F32) + dot(lon_t[...], g)).astype(BF)
    w1[...] = sums[:12, :192]
    w2[...] = sums[:12, 192:]
    b1[...] = sums[12:14, :12]
    b2[...] = sums[14:, :12]


def shards(tables, lon_t, tokens, cotangent, w_first, b_first, w_second, b_second):
    blocks = lambda n, kind: pltpu.VMEM((n, 16, 384), kind)
    parts = lambda kind: pltpu.VMEM((4, 256, 384), kind)
    loaded = [(2, 384, 768), (2, 384, 768), (192, 768), (2, 768), (192, 768), (2, 768)]
    scratch = [pltpu.VMEM(n, BF) for n in loaded] + [pltpu.VMEM(t.shape, BF) for t in tables]
    scratch += [
        pltpu.SemaphoreType.DMA((14,)),
        pltpu.VMEM((2, 2, 256, 384), F32),
        blocks(64, BF), pltpu.VMEM((64, 1, 128), F32), blocks(64, BF), pltpu.VMEM((64, 1, 128), F32),
        pltpu.VMEM((64, 16, 256), BF), pltpu.VMEM((64, 16, 256), BF), pltpu.VMEM((64, 16, 128), BF), pltpu.VMEM((64, 16, 128), BF),
        pltpu.VMEM((64, 16, 128), BF), pltpu.VMEM((64, 16, 256), BF),
        pltpu.VMEM((4, 256, 128), F32),
        pltpu.VMEM((3, 1024, 128), F32),
        parts(BF), parts(BF), parts(BF), parts(BF),
        pltpu.VMEM((1024, 384), BF), pltpu.VMEM((1024, 384), BF),
        pltpu.VMEM((384, 768), BF), pltpu.VMEM((384, 768), BF),
        pltpu.VMEM((4, 512, 256), BF), pltpu.VMEM((4, 512, 256), BF), pltpu.VMEM((4, 4, 256, 384), BF),
        pltpu.VMEM((16, 4, 8, 384), F32), pltpu.VMEM((16, 4, 8, 384), F32),
        pltpu.VMEM((4, 8, 384), F32), pltpu.VMEM((4, 8, 384), F32),
        pltpu.VMEM((1, 8, 384), F32), pltpu.VMEM((8, 8, 384), F32),
        pltpu.SemaphoreType.DMA((9,)), pltpu.SemaphoreType.DMA((9,)),
    ]
    spec = pl.BlockSpec(memory_space=pl.ANY)
    first, second, sums = pl.pallas_call(
        kernel,
        out_shape=(
            jax.ShapeDtypeStruct((64, 16, 128), BF),
            jax.ShapeDtypeStruct((64, 16, 256), BF),
            jax.ShapeDtypeStruct((16, 384), F32),
        ),
        in_specs=[spec] * 12,
        out_specs=(spec, spec, pl.BlockSpec(memory_space=pltpu.VMEM)),
        scratch_shapes=scratch,
        name="afno_backward",
        compiler_params=pltpu.CompilerParams(
            collective_id=0, has_side_effects=True, vmem_limit_bytes=60 << 20
        ),
    )(tokens[0], cotangent[0], w_first.T, b_first, w_second.T, b_second, *[jnp.asarray(t) for t in tables])
    whole = lambda *shape: pl.BlockSpec(shape, lambda f: (0,) * len(shape))
    field = lambda: pl.BlockSpec((2, 384, 384), lambda f: (0, 0, f))
    part = lambda lanes: pl.BlockSpec((32, 16, lanes), lambda f: (f, 0, 0))
    out, w1, b1, w2, b2 = pl.pallas_call(
        finish,
        grid=(2,),
        out_shape=(
            jax.ShapeDtypeStruct((2, 384, 768), BF),
            jax.ShapeDtypeStruct((12, 192), F32),
            jax.ShapeDtypeStruct((2, 12), F32),
            jax.ShapeDtypeStruct((12, 192), F32),
            jax.ShapeDtypeStruct((2, 12), F32),
        ),
        in_specs=[field(), part(128), part(256), whole(16, 384), whole(384, 256)],
        out_specs=(field(), whole(12, 192), whole(2, 12), whole(12, 192), whole(2, 12)),
        name="finish",
        compiler_params=pltpu.CompilerParams(vmem_limit_bytes=60 << 20),
    )(cotangent[0], first, second, sums, jnp.asarray(lon_t))
    return out[None], w1, b1, w2, b2


def solution(mesh):
    return jax.shard_map(
        functools.partial(shards, *constants()),
        mesh=mesh,
        in_specs=(P("ens", "sp", None, None), P("ens", "sp", None, None), P(), P(), P(), P()),
        out_specs=(
            P("ens", "sp", None, None),
            P("sp", None),
            P(None, "sp"),
            P("sp", None),
            P(None, "sp"),
        ),
        check_vma=False,
    )
```
